32 devices in a mesh: space: 8 (over z, core), samp: 4 (over y, x).
Axes of the slice: x: 2, y: 2, z: 4, core: 2. Of those that a mesh axis runs over, the one named last changes fastest.
Arguments:
- basis_u: bfloat16 [128, 16, 8, 128], P('samp', 'space'), may hold values from -0.75 to 0.75
- basis_v: bfloat16 [128, 32768], P('space', 'samp'), may hold values from -0.75 to 0.75
- core_s: float32 [128, 128], replicated, may hold values from -4 to 4
- face_class: int32 [6, 16, 8, 128], P(None, 'space'), may hold values from 0 to 3
- sample_class: int32 [32768], P('samp'), may hold values from 0 to 3
Outputs:
- k_new: float32 [128, 16, 8, 128], P('samp', 'space')
- l_new: float32 [128, 32768], P('space', 'samp')
The draws below stay inside these ranges and needn't reach their ends.
All inputs are finite; a program needn't handle non-finite values.
Results may differ from the reference program's by a relative error of at most 0.0046.
Values may be sent and summed in bfloat16 or wider, within the bound.
A program may use at most 64 MiB of HBM per device.

```python
import jax
import jax.numpy as jnp
from jax import lax

NY = 8
NZ = 128
R = 128
NX = 16
CELLS = 16384
NSAMP = 32768


def place_ends(drawn, stream_key, smallest, largest):
    extent = drawn.shape
    spot = [jax.random.randint(jax.random.fold_in(stream_key, axis), (), 0, extent[axis]) for axis in range(len(extent))]
    drawn = drawn.at[tuple(spot)].set(smallest)
    longest = extent.index(max(extent))
    spot[longest] = (spot[longest] + 1) % extent[longest]
    return drawn.at[tuple(spot)].set(largest)


def raised(entries, rng, source, target, parts, factor):
    owner, partner = [(jnp.arange(entries.shape[position]) // (entries.shape[position] // parts)).reshape([-1 if axis == position else 1 for axis in range(entries.ndim)]) for position in (source, target)]
    chosen = jax.random.permutation(rng, parts)[partner]
    strong = (owner == chosen) | (owner == (partner + parts // 2) % parts)
    return jnp.where(strong, factor * entries, entries)


def level_of(own_key, shape, pieces, low, top_value):
    loudness, own = 1.0, jax.random.fold_in(own_key, 6)
    for position, shards_of in pieces:
        steps = jnp.exp(jax.random.uniform(jax.random.fold_in(own, position), (shards_of,), jnp.float32, low / len(pieces), top_value / len(pieces)))
        loudness = loudness * jnp.repeat(steps, shape[position] // shards_of).reshape([-1 if axis == position else 1 for axis in range(len(shape))])
    return loudness


def centred(stream_key, shape, scale, most, cuts=(), kind=jnp.bfloat16):
    gain = level_of(stream_key, shape, cuts, -0.22, 0.18) if cuts else 1.0
    result = jax.random.normal(stream_key, shape, jnp.float32) * scale * gain
    return jnp.minimum(jnp.maximum(result, -most), most).astype(kind)


def heavy_noise(own_key, extent, scale, bound, cuts, heavy, held_as=jnp.bfloat16):
    values = scale * jax.random.normal(own_key, extent, jnp.float32)
    if cuts:
        values = values * level_of(own_key, extent, cuts, -0.22, 0.18)
    return jnp.clip(raised(values, jax.random.fold_in(own_key, 3), *heavy), -bound, bound).astype(held_as)


def setup_inputs(seed: int = 0) -> dict:
    splits = jax.random.split(jax.random.key(seed), 6)
    basis_u = heavy_noise(splits[0], (R, NX, NY, NZ), R ** -0.5, 0.75, ((0, 4), (1, 8)), (1, 0, 8, 2.0))
    basis_v = heavy_noise(splits[1], (R, NSAMP), R ** -0.5, 0.75, ((0, 8), (1, 4)), (1, 0, 8, 2.0))
    core_s = centred(splits[2], (R, R), 1.0, 4.0, (), jnp.float32)
    face_class = place_ends(jax.random.randint(splits[3], (6, NX, NY, NZ), 0, 4), jax.random.fold_in(splits[3], 1), 0, 3).astype(jnp.int32)
    sample_class = place_ends(jax.random.randint(splits[4], (NSAMP,), 0, 4), jax.random.fold_in(splits[4], 1), 0, 3).astype(jnp.int32)
    return {"basis_u": basis_u, "basis_v": basis_v, "core_s": core_s, "face_class": face_class, "sample_class": sample_class}


step_size = 0.1


def laplace_of(k_old, face_class):
    weight = 0.25 * jnp.exp2(face_class.astype(jnp.float32))[..., None]
    padded_grid = jnp.pad(k_old.astype(jnp.float32), ((1, 1), (1, 1), (1, 1), (0, 0)))
    centre = padded_grid[1:-1, 1:-1, 1:-1]
    beside_all = (padded_grid[:-2, 1:-1, 1:-1], padded_grid[2:, 1:-1, 1:-1],
              padded_grid[1:-1, :-2, 1:-1], padded_grid[1:-1, 2:, 1:-1],
              padded_grid[1:-1, 1:-1, :-2], padded_grid[1:-1, 1:-1, 2:])
    summed = jnp.zeros_like(centre)
    for side_index in range(6):
        summed = summed + weight[side_index] * (beside_all[side_index] - centre)
    return summed


def reference(basis_u, basis_v, core_s, face_class, sample_class):
    core_b = core_s.astype(jnp.bfloat16)
    u_rows = basis_u.reshape(R, -1).T
    v_rows = basis_v.T
    k_flat = jnp.dot(u_rows, core_b, preferred_element_type=jnp.float32).astype(jnp.bfloat16)
    k_old = k_flat.reshape(NX, NY, NZ, R)
    laplace = laplace_of(k_old, face_class)
    lap_b = laplace.reshape(-1, R).astype(jnp.bfloat16)
    growth = 0.5 + 0.5 * sample_class.astype(jnp.float32)
    block_rows = min(512, NSAMP)
    block_count = NSAMP // block_rows
    v_blocks = v_rows.reshape(block_count, block_rows, R)
    g_blocks = growth.reshape(block_count, block_rows)

    def tile_step(accumulated, block_pair):
        v_block, g_block = block_pair
        sample_field = lax.dot_general(k_flat, v_block, (((1,), (1,)), ((), ())), preferred_element_type=jnp.float32)
        reaction = (g_block[None, :] * sample_field - sample_field * sample_field * sample_field).astype(jnp.bfloat16)
        accumulated = accumulated + jnp.dot(reaction, v_block, preferred_element_type=jnp.float32)
        onto_u = lax.dot_general(reaction, u_rows, (((0,), (0,)), ((), ())), preferred_element_type=jnp.float32)
        return accumulated, onto_u

    start_acc = jnp.zeros((CELLS, R), jnp.float32)
    accumulated, onto_blocks = lax.scan(tile_step, start_acc, (v_blocks, g_blocks))
    k_proj = accumulated * (R / NSAMP)
    k_cells = k_old.astype(jnp.float32) + step_size * (laplace + k_proj.reshape(NX, NY, NZ, R))
    moment = lax.dot_general(u_rows, lap_b, (((0,), (0,)), ((), ())), preferred_element_type=jnp.float32) * (R / CELLS)
    l_old = lax.dot_general(v_rows, core_b, (((1,), (1,)), ((), ())), preferred_element_type=jnp.float32)
    l_proj = onto_blocks.reshape(NSAMP, R) * (R / CELLS)
    side_term = jnp.dot(v_rows.astype(jnp.float32), moment.T, precision=lax.Precision.HIGHEST)
    l_rows = l_old + step_size * (side_term + l_proj)
    return jnp.transpose(k_cells, (3, 0, 1, 2)), l_rows.T
```

```python
import functools

import jax
import jax.numpy as jnp
from jax import lax
from jax.experimental import pallas as pl
from jax.experimental.pallas import tpu as pltpu
from jax.sharding import PartitionSpec as P

step_size = 0.1
f32 = jnp.float32
bf16 = jnp.bfloat16


def dot(a, b, dims):
    return lax.dot_general(a, b, (dims, ((), ())), preferred_element_type=f32)


def joined(blocks):
    n, rows, columns = blocks.shape
    if rows % 16 == 0:
        return blocks.reshape(n * rows, columns)
    return blocks.astype(f32).reshape(n * rows, columns).astype(blocks.dtype)


def kernel(
    dims, u_ref, v_ref, core_ref, core_cols_ref, weight_ref, class_ref,
    k_out, l_out,
    u_all, v_all, k_rows, k_mine, halo_lo, halo_hi, lap, k_acc, react,
    m_parts, m_all, m_full, l_part, l_sib, l_sum, l_recv, k_part, k_recv,
    u_s, u_r, v_s, v_r, w_s, w_r, h_s, h_r, m_s, m_r, n_s, n_r,
    a_s, a_r, b_s, b_r, c_s, c_r,
):
    n_space, n_samp, n_chunks, chunk, tile, cell_tile, depth_x, rows_y, cols_z = dims
    n_chip = n_space // 2
    narrow, cells = u_ref.shape
    lane_width, samples = v_ref.shape
    rank = n_samp * narrow
    plane = rows_y * cols_z
    cell_scale = step_size * rank / (cells * n_space)
    samp_scale = rank / (samples * n_samp)

    me = lax.axis_index("space")
    col = lax.axis_index("samp")
    chip, core = me // 2, me % 2
    other = 1 - core

    def space_peer(k):
        return lax.rem(me + k, n_space)

    def samp_peer(k):
        return lax.rem(col + k, n_samp)

    def chip_peer(k):
        return lax.rem(chip + k, n_chip)

    def chip_before(k):
        return lax.rem(chip - k + n_chip, n_chip)

    def remote(src, dst, send, recv, where):
        return pltpu.make_async_remote_copy(
            src_ref=src, dst_ref=dst, send_sem=send, recv_sem=recv,
            device_id=where, device_id_type=pl.DeviceIdType.MESH,
        )

    def at_chunk(c):
        return pl.ds(pl.multiple_of(c * chunk, chunk), chunk)

    def to_sibling():
        return {"space": chip * 2 + other}

    def u_copy(k, slot):
        return remote(u_ref, u_all.at[slot], u_s.at[k], u_r.at[k], {"samp": samp_peer(k)})

    def v_copy(k, c, slot):
        return remote(
            v_ref.at[:, at_chunk(c)], v_all.at[slot, :, at_chunk(c)],
            v_s.at[k, c], v_r.at[k, c], {"space": chip_peer(k) * 2 + core},
        )

    def v_own(c, slot):
        return remote(
            v_ref.at[:, at_chunk(c)], v_all.at[slot, :, at_chunk(c)],
            w_s.at[0, c], w_r.at[0, c], to_sibling(),
        )

    def v_forward(k, c, slot):
        return remote(
            v_all.at[slot, :, at_chunk(c)], v_all.at[slot, :, at_chunk(c)],
            w_s.at[k, c], w_r.at[k, c], to_sibling(),
        )

    def l_swap(c):
        return remote(
            l_part.at[other, :, :, at_chunk(c)], l_sib.at[:, :, at_chunk(c)],
            a_s.at[c], a_r.at[c], to_sibling(),
        )

    def l_copy(k, c):
        return remote(
            l_sum.at[chip_peer(k), :, at_chunk(c)], l_recv.at[k - 1, :, at_chunk(c)],
            b_s.at[k, c], b_r.at[k, c], {"space": chip_peer(k) * 2 + core},
        )

    def m_copy(k, slot):
        return remote(m_parts.at[me], m_parts.at[slot], m_s.at[k], m_r.at[k], {"space": space_peer(k)})

    def m_share(k, slot):
        return remote(m_all.at[col], m_all.at[slot], n_s.at[k], n_r.at[k], {"samp": samp_peer(k)})

    def k_copy(k):
        return remote(k_part.at[samp_peer(k)], k_recv.at[k - 1], c_s.at[k], c_r.at[k], {"samp": samp_peer(k)})

    def halo_up():
        return remote(k_mine.at[:, pl.ds(cells - plane, plane)], halo_lo, h_s.at[0], h_r.at[0], {"space": space_peer(1)})

    def halo_down():
        return remote(k_mine.at[:, pl.ds(0, plane)], halo_hi, h_s.at[1], h_r.at[1], {"space": space_peer(n_space - 1)})

    barrier = pltpu.get_barrier_semaphore()
    for k in range(1, n_space):
        pl.semaphore_signal(barrier, inc=1, device_id={"space": space_peer(k)}, device_id_type=pl.DeviceIdType.MESH)
    for k in range(1, n_samp):
        pl.semaphore_signal(barrier, inc=1, device_id={"samp": samp_peer(k)}, device_id_type=pl.DeviceIdType.MESH)
    pl.semaphore_wait(barrier, n_space + n_samp - 2)

    for k in range(1, n_samp):
        u_copy(k, col).start()

    def send_v(c, carry):
        for k in range(1, n_chip):
            v_copy(k, c, me).start()
        v_own(c, me).start()
        return carry

    lax.fori_loop(0, n_chunks, send_v, 0)

    u_all[col] = u_ref[...]
    v_all[me] = v_ref[...]
    k_acc[...] = jnp.zeros_like(k_acc)

    for k in range(1, n_samp):
        u_copy(k, lax.rem(col - k + n_samp, n_samp)).wait_recv()

    core_b = core_ref[...].astype(bf16)
    for first in range(0, cells, cell_tile):
        spot = slice(first, first + cell_tile)
        u_tile = joined(u_all[:, :, spot])
        k_rows[spot, :] = dot(u_tile, core_b, ((0,), (0,))).astype(bf16)
        k_mine[:, spot] = dot(core_cols_ref[...], u_tile, ((1,), (0,))).astype(bf16)

    @pl.when(me < n_space - 1)
    def _():
        halo_up().start()

    @pl.when(me > 0)
    def _():
        halo_down().start()

    def forward(c):
        for k in range(1, n_chip):
            slot = chip_before(k) * 2 + core
            v_copy(k, c, slot).wait_recv()
            v_forward(k, c, slot).start()

    def await_sibling(c):
        v_own(c, chip * 2 + other).wait_recv()
        for k in range(1, n_chip):
            v_forward(k, c, chip_before(k) * 2 + other).wait_recv()

    def compute(c, part):
        spot = pl.ds(pl.multiple_of(c * chunk + part * tile, tile), tile)
        v = joined(v_all[:, :, spot])
        growth = 0.5 + 0.5 * class_ref[:, spot].astype(f32)
        for first in range(0, cells, cell_tile):
            rows = slice(first, first + cell_tile)
            field = dot(k_rows[rows, :], v, ((1,), (0,)))
            reaction = (field * (growth - field * field)).astype(bf16)
            react[rows, :] = reaction
            k_acc[rows, :] += dot(reaction, v, ((1,), (1,)))
        u_full = joined(u_all[...])
        onto_u = dot(u_full, react[...], ((1,), (0,))).astype(bf16)
        for place in range(n_chip):
            for side in range(2):
                row = (2 * place + side) * lane_width
                l_part[side, place, :, spot] = onto_u[row:row + lane_width, :]

    def chip_sum(c):
        l_swap(c).wait_recv()
        spot = at_chunk(c)
        l_sum[:, :, spot] = (l_part[core, :, :, spot].astype(f32) + l_sib[:, :, spot].astype(f32)).astype(bf16)
        for k in range(1, n_chip):
            l_copy(k, c).start()

    def stencil():
        @pl.when(me > 0)
        def _():
            halo_up().wait_recv()

        @pl.when(me == 0)
        def _():
            halo_lo[...] = jnp.zeros_like(halo_lo)

        @pl.when(me < n_space - 1)
        def _():
            halo_down().wait_recv()

        @pl.when(me == n_space - 1)
        def _():
            halo_hi[...] = jnp.zeros_like(halo_hi)

        lane = lax.broadcasted_iota(jnp.int32, (narrow, cols_z), 1)
        nothing = jnp.zeros((narrow, cols_z), f32)

        def line(ref, first):
            return ref[:, first:first + cols_z].astype(f32)

        for x in range(depth_x):
            for y in range(rows_y):
                at = (x * rows_y + y) * cols_z
                centre = line(k_mine, at)
                beside = (
                    line(k_mine, at - plane) if x > 0 else line(halo_lo, y * cols_z),
                    line(k_mine, at + plane) if x < depth_x - 1 else line(halo_hi, y * cols_z),
                    line(k_mine, at - cols_z) if y > 0 else nothing,
                    line(k_mine, at + cols_z) if y < rows_y - 1 else nothing,
                    jnp.where(lane == 0, 0.0, pltpu.roll(centre, 1, 1)),
                    jnp.where(lane == cols_z - 1, 0.0, pltpu.roll(centre, cols_z - 1, 1)),
                )
                summed = nothing
                for face in range(6):
                    summed = summed + weight_ref[face:face + 1, at:at + cols_z] * (beside[face] - centre)
                lap[:, at:at + cols_z] = summed
        m_parts[me] = dot(lap[...].astype(bf16), joined(u_all[...]), ((1,), (1,)))
        for k in range(1, n_space):
            m_copy(k, me).start()

    def moment_sum():
        for k in range(1, n_space):
            m_copy(k, lax.rem(me - k + n_space, n_space)).wait_recv()
        total = m_parts[0]
        for k in range(1, n_space):
            total = total + m_parts[k]
        m_all[col] = total
        for k in range(1, n_samp):
            m_share(k, col).start()

    def moment_rows():
        for k in range(1, n_samp):
            m_share(k, lax.rem(col - k + n_samp, n_samp)).wait_recv()
        moment = m_all[...].reshape(rank, rank).T
        m_full[...] = core_ref[...].astype(bf16).astype(f32) + cell_scale * moment

    def finish_l(c):
        spot = at_chunk(c)
        for k in range(1, n_chip):
            l_copy(k, c).wait_recv()
        total = l_sum[chip, :, spot].astype(f32)
        for k in range(1, n_chip):
            total = total + l_recv[k - 1, :, spot].astype(f32)
        mine = m_full[pl.ds(pl.multiple_of(me * lane_width, lane_width), lane_width), :]
        high = mine.astype(bf16)
        low = (mine - high.astype(f32)).astype(bf16)
        v = joined(v_all[:, :, spot])
        l_out[:, spot] = dot(high, v, ((1,), (0,))) + dot(low, v, ((1,), (0,))) + cell_scale * total

    forward(0)
    await_sibling(0)
    parts = chunk // tile

    def step(c, carry):
        compute(c, 0)

        @pl.when(c + 1 < n_chunks)
        def _():
            forward(c + 1)

        @pl.when(c > 0)
        def _():
            chip_sum(c - 1)

        for part in range(1, parts):
            compute(c, part)
        l_swap(c).start()

        for place, task in enumerate((stencil, moment_sum, moment_rows)):
            pl.when(c == min(place, n_chunks - 1))(task)

        @pl.when(c > 1)
        def _():
            finish_l(c - 2)

        @pl.when(c + 1 < n_chunks)
        def _():
            await_sibling(c + 1)

        return carry

    lax.fori_loop(0, n_chunks, step, 0)

    for first in range(0, cells, cell_tile):
        spot = slice(first, first + cell_tile)
        turned = (k_acc[spot, :].T * samp_scale).astype(bf16)
        for place in range(n_samp):
            k_part[place, :, spot] = turned[place * narrow:(place + 1) * narrow, :]
    for k in range(1, n_samp):
        k_copy(k).start()
    chip_sum(n_chunks - 1)
    if n_chunks > 1:
        finish_l(n_chunks - 2)
    for k in range(1, n_samp):
        k_copy(k).wait_recv()
    total = k_part[col].astype(f32)
    for k in range(1, n_samp):
        total = total + k_recv[k - 1].astype(f32)
    k_out[...] = k_mine[...].astype(f32) + step_size * (lap[...] + total)
    finish_l(n_chunks - 1)

    for k in range(1, n_samp):
        u_copy(k, col).wait_send()
        m_share(k, col).wait_send()
        k_copy(k).wait_send()
    for k in range(1, n_space):
        m_copy(k, me).wait_send()

    @pl.when(me < n_space - 1)
    def _():
        halo_up().wait_send()

    @pl.when(me > 0)
    def _():
        halo_down().wait_send()

    def sent(c, carry):
        for k in range(1, n_chip):
            v_copy(k, c, me).wait_send()
            v_forward(k, c, chip_before(k) * 2 + core).wait_send()
            l_copy(k, c).wait_send()
        v_own(c, me).wait_send()
        l_swap(c).wait_send()
        return carry

    lax.fori_loop(0, n_chunks, sent, 0)


def per_device(basis_u, basis_v, core_s, face_class, sample_class):
    n_space = lax.axis_size("space")
    n_samp = lax.axis_size("samp")
    narrow, depth_x, rows_y, cols_z = basis_u.shape
    rank = core_s.shape[0]
    lane_width, samples = basis_v.shape
    cells = depth_x * rows_y * cols_z
    plane = rows_y * cols_z
    n_chip = n_space // 2
    chunk = min(1024, samples)
    tile = min(512, chunk)
    cell_tile = min(512, cells)
    n_chunks = samples // chunk
    core_cols = lax.dynamic_slice_in_dim(
        core_s.astype(bf16).T, lax.axis_index("samp") * narrow, narrow, 0
    )
    weight = 0.25 * jnp.exp2(face_class.astype(f32)).reshape(face_class.shape[0], cells)
    dims = (n_space, n_samp, n_chunks, chunk, tile, cell_tile, depth_x, rows_y, cols_z)
    dma = pltpu.SemaphoreType.DMA
    vmem = pl.BlockSpec(memory_space=pltpu.VMEM)
    k_new, l_new = pl.pallas_call(
        functools.partial(kernel, dims),
        out_shape=(
            jax.ShapeDtypeStruct((narrow, cells), f32),
            jax.ShapeDtypeStruct((lane_width, samples), f32),
        ),
        in_specs=[vmem] * 6,
        out_specs=(vmem, vmem),
        scratch_shapes=[
            pltpu.VMEM((n_samp, narrow, cells), bf16),
            pltpu.VMEM((n_space, lane_width, samples), bf16),
            pltpu.VMEM((cells, rank), bf16),
            pltpu.VMEM((narrow, cells), bf16),
            pltpu.VMEM((narrow, plane), bf16),
            pltpu.VMEM((narrow, plane), bf16),
            pltpu.VMEM((narrow, cells), f32),
            pltpu.VMEM((cells, rank), f32),
            pltpu.VMEM((cells, tile), bf16),
            pltpu.VMEM((n_space, narrow, rank), f32),
            pltpu.VMEM((n_samp, narrow, rank), f32),
            pltpu.VMEM((rank, rank), f32),
            pltpu.VMEM((2, n_chip, lane_width, samples), bf16),
            pltpu.VMEM((n_chip, lane_width, samples), bf16),
            pltpu.VMEM((n_chip, lane_width, samples), bf16),
            pltpu.VMEM((n_chip - 1, lane_width, samples), bf16),
            pltpu.VMEM((n_samp, narrow, cells), bf16),
            pltpu.VMEM((n_samp - 1, narrow, cells), bf16),
            dma((n_samp,)), dma((n_samp,)),
            dma((n_chip, n_chunks)), dma((n_chip, n_chunks)),
            dma((n_chip, n_chunks)), dma((n_chip, n_chunks)),
            dma((2,)), dma((2,)),
            dma((n_space,)), dma((n_space,)),
            dma((n_samp,)), dma((n_samp,)),
            dma((n_chunks,)), dma((n_chunks,)),
            dma((n_chip, n_chunks)), dma((n_chip, n_chunks)),
            dma((n_samp,)), dma((n_samp,)),
        ],
        compiler_params=pltpu.CompilerParams(
            collective_id=0, has_side_effects=True, vmem_limit_bytes=48 * 1024 * 1024
        ),
        cost_estimate=pl.CostEstimate(
            flops=6 * cells * samples * rank, bytes_accessed=2 * rank * samples, transcendentals=0
        ),
    )(
        basis_u.reshape(narrow, cells), basis_v, core_s, core_cols, weight,
        sample_class.reshape(1, samples),
    )
    return (k_new.reshape(narrow, depth_x, rows_y, cols_z), l_new)


def solution(mesh):
    placed = (
        P("samp", "space", None, None),
        P("space", "samp"),
        P(),
        P(None, "space", None, None),
        P("samp"),
    )
    return jax.shard_map(
        per_device,
        mesh=mesh,
        in_specs=placed,
        out_specs=(P("samp", "space", None, None), P("space", "samp")),
        check_vma=False,
    )
```

```python
import functools

import jax
import jax.numpy as jnp
from jax import lax
from jax.experimental import pallas as pl
from jax.experimental.pallas import tpu as pltpu
from jax.sharding import PartitionSpec as P

step_size = 0.1
f32 = jnp.float32
bf16 = jnp.bfloat16


def dot(a, b, dims):
    return lax.dot_general(a, b, (dims, ((), ())), preferred_element_type=f32)


def joined(blocks):
    n, rows, columns = blocks.shape
    if rows % 16 == 0:
        return blocks.reshape(n * rows, columns)
    return blocks.astype(f32).reshape(n * rows, columns).astype(blocks.dtype)


def kernel(
    dims, u_ref, v_ref, core_ref, core_cols_ref, weight_ref, class_ref,
    k_out, l_out,
    u_all, v_all, k_rows, k_mine, halo_lo, halo_hi, lap, k_acc, react,
    m_parts, m_all, m_full, l_part, l_sib, l_sum, l_recv, l_out_line, l_in_line, k_part, k_recv,
    u_s, u_r, v_s, v_r, w_s, w_r, h_s, h_r, m_s, m_r, n_s, n_r,
    a_s, a_r, b_s, b_r, c_s, c_r, d_s, d_r,
):
    n_space, n_samp, n_chunks, chunk, tile, cell_tile, depth_x, rows_y, cols_z = dims
    n_chip = n_space // 2
    n_line = max(0, n_chunks - 2)
    narrow, cells = u_ref.shape
    lane_width, samples = v_ref.shape
    rank = n_samp * narrow
    plane = rows_y * cols_z
    cell_scale = step_size * rank / (cells * n_space)
    samp_scale = rank / (samples * n_samp)

    me = lax.axis_index("space")
    col = lax.axis_index("samp")
    chip, core = me // 2, me % 2
    other = 1 - core

    def space_peer(k):
        return lax.rem(me + k, n_space)

    def samp_peer(k):
        return lax.rem(col + k, n_samp)

    def chip_peer(k):
        return lax.rem(chip + k, n_chip)

    def chip_before(k):
        return lax.rem(chip - k + n_chip, n_chip)

    def remote(src, dst, send, recv, where):
        return pltpu.make_async_remote_copy(
            src_ref=src, dst_ref=dst, send_sem=send, recv_sem=recv,
            device_id=where, device_id_type=pl.DeviceIdType.MESH,
        )

    def at_chunk(c):
        return pl.ds(pl.multiple_of(c * chunk, chunk), chunk)

    def to_sibling():
        return {"space": chip * 2 + other}

    def u_copy(k, slot):
        return remote(u_ref, u_all.at[slot], u_s.at[k], u_r.at[k], {"samp": samp_peer(k)})

    def toward(side):
        return lax.rem(chip + (1 if side == 0 else n_chip - 1), n_chip)

    def held(side, k):
        return chip >= k if side == 0 else chip + k < n_chip

    def goes_on(side):
        return chip < n_chip - 1 if side == 0 else chip > 0

    def origin(side, k):
        return lax.rem(chip + (n_chip - k if side == 0 else k), n_chip)

    def v_line(side, k, c):
        slot = origin(side, k) * 2 + core
        block = v_all.at[slot, :, at_chunk(c)]
        return remote(
            v_ref.at[:, at_chunk(c)] if k == 0 else block, block,
            v_s.at[side, k, c], v_r.at[side, k + 1, c], {"space": toward(side) * 2 + core},
        )

    def v_arrival(side, k, c):
        block = v_all.at[origin(side, k) * 2 + core, :, at_chunk(c)]
        return remote(
            block, block, v_s.at[side, k - 1, c], v_r.at[side, k, c],
            {"space": toward(side) * 2 + core},
        )

    def v_own(c, slot):
        return remote(
            v_ref.at[:, at_chunk(c)], v_all.at[slot, :, at_chunk(c)],
            w_s.at[0, 0, c], w_r.at[0, 0, c], to_sibling(),
        )

    def v_forward(side, k, c, which):
        block = v_all.at[origin(side, k) * 2 + which, :, at_chunk(c)]
        return remote(block, block, w_s.at[side, k, c], w_r.at[side, k, c], to_sibling())

    def l_line(side, target, c):
        return remote(
            l_out_line.at[side, target, :, at_chunk(c)], l_in_line.at[side, target, :, at_chunk(c)],
            d_s.at[side, target, c], d_r.at[side, target, c], {"space": toward(side) * 2 + core},
        )

    def l_swap(c):
        return remote(
            l_part.at[other, :, :, at_chunk(c)], l_sib.at[:, :, at_chunk(c)],
            a_s.at[c], a_r.at[c], to_sibling(),
        )

    def l_copy(k, c):
        return remote(
            l_sum.at[chip_peer(k), :, at_chunk(c)], l_recv.at[k - 1, :, at_chunk(c)],
            b_s.at[k, c], b_r.at[k, c], {"space": chip_peer(k) * 2 + core},
        )

    def m_copy(k, slot):
        return remote(m_parts.at[me], m_parts.at[slot], m_s.at[k], m_r.at[k], {"space": space_peer(k)})

    def m_share(k, slot):
        return remote(m_all.at[col], m_all.at[slot], n_s.at[k], n_r.at[k], {"samp": samp_peer(k)})

    def k_copy(k):
        return remote(k_part.at[samp_peer(k)], k_recv.at[k - 1], c_s.at[k], c_r.at[k], {"samp": samp_peer(k)})

    def halo_up():
        return remote(k_mine.at[:, pl.ds(cells - plane, plane)], halo_lo, h_s.at[0], h_r.at[0], {"space": space_peer(1)})

    def halo_down():
        return remote(k_mine.at[:, pl.ds(0, plane)], halo_hi, h_s.at[1], h_r.at[1], {"space": space_peer(n_space - 1)})

    barrier = pltpu.get_barrier_semaphore()
    for k in range(1, n_space):
        pl.semaphore_signal(barrier, inc=1, device_id={"space": space_peer(k)}, device_id_type=pl.DeviceIdType.MESH)
    for k in range(1, n_samp):
        pl.semaphore_signal(barrier, inc=1, device_id={"samp": samp_peer(k)}, device_id_type=pl.DeviceIdType.MESH)
    pl.semaphore_wait(barrier, n_space + n_samp - 2)

    for k in range(1, n_samp):
        u_copy(k, col).start()

    def wave(w):
        for k in range(n_chip):
            c = w - k

            @pl.when((c >= 0) & (c < n_chunks))
            def _():
                for side in range(2):
                    if k > 0:
                        @pl.when(held(side, k))
                        def _():
                            v_arrival(side, k, c).wait_recv()

                            @pl.when(goes_on(side))
                            def _():
                                v_line(side, k, c).start()

                            v_forward(side, k, c, core).start()
                    else:
                        @pl.when(goes_on(side))
                        def _():
                            v_line(side, k, c).start()
                if k == 0:
                    v_own(c, me).start()

    wave(0)
    u_all[col] = u_ref[...]
    v_all[me] = v_ref[...]
    k_acc[...] = jnp.zeros_like(k_acc)
    for side in range(2):
        @pl.when(chip == (0 if side == 0 else n_chip - 1))
        def _():
            l_in_line[side] = jnp.zeros_like(l_in_line[side])
    wave(1)
    wave(2)

    for k in range(1, n_samp):
        u_copy(k, lax.rem(col - k + n_samp, n_samp)).wait_recv()

    core_b = core_ref[...].astype(bf16)
    for first in range(0, cells, cell_tile):
        spot = slice(first, first + cell_tile)
        u_tile = joined(u_all[:, :, spot])
        k_rows[spot, :] = dot(u_tile, core_b, ((0,), (0,))).astype(bf16)
        k_mine[:, spot] = dot(core_cols_ref[...], u_tile, ((1,), (0,))).astype(bf16)

    @pl.when(me < n_space - 1)
    def _():
        halo_up().start()

    @pl.when(me > 0)
    def _():
        halo_down().start()

    def await_sibling(c):
        v_own(c, chip * 2 + other).wait_recv()
        for side in range(2):
            for k in range(1, n_chip):
                @pl.when(held(side, k))
                def _():
                    v_forward(side, k, c, other).wait_recv()

    def compute(c, part):
        spot = pl.ds(pl.multiple_of(c * chunk + part * tile, tile), tile)
        v = joined(v_all[:, :, spot])
        growth = 0.5 + 0.5 * class_ref[:, spot].astype(f32)
        for first in range(0, cells, cell_tile):
            rows = slice(first, first + cell_tile)
            field = dot(k_rows[rows, :], v, ((1,), (0,)))
            reaction = (field * (growth - field * field)).astype(bf16)
            react[rows, :] = reaction
            k_acc[rows, :] += dot(reaction, v, ((1,), (1,)))
        u_full = joined(u_all[...])
        onto_u = dot(u_full, react[...], ((1,), (0,))).astype(bf16)
        for place in range(n_chip):
            for side in range(2):
                row = (2 * place + side) * lane_width
                l_part[side, place, :, spot] = onto_u[row:row + lane_width, :]

    def chip_sum(c):
        l_swap(c).wait_recv()
        spot = at_chunk(c)
        l_sum[:, :, spot] = (l_part[core, :, :, spot].astype(f32) + l_sib[:, :, spot].astype(f32)).astype(bf16)

        @pl.when(c >= n_line)
        def _():
            for k in range(1, n_chip):
                l_copy(k, c).start()

    def line_sums(t):
        for side in range(2):
            c = t - 1 - (chip if side == 0 else n_chip - 1 - chip)

            @pl.when((c >= 0) & (c < n_line))
            def _():
                spot = at_chunk(c)
                for target in range(n_chip):
                    @pl.when(chip < target if side == 0 else chip > target)
                    def _():
                        @pl.when(chip > 0 if side == 0 else chip < n_chip - 1)
                        def _():
                            l_line(side, target, c).wait_recv()

                        l_out_line[side, target, :, spot] = (
                            l_sum[target, :, spot].astype(f32) + l_in_line[side, target, :, spot].astype(f32)
                        ).astype(bf16)
                        l_line(side, target, c).start()

    def stencil():
        @pl.when(me > 0)
        def _():
            halo_up().wait_recv()

        @pl.when(me == 0)
        def _():
            halo_lo[...] = jnp.zeros_like(halo_lo)

        @pl.when(me < n_space - 1)
        def _():
            halo_down().wait_recv()

        @pl.when(me == n_space - 1)
        def _():
            halo_hi[...] = jnp.zeros_like(halo_hi)

        lane = lax.broadcasted_iota(jnp.int32, (narrow, cols_z), 1)
        nothing = jnp.zeros((narrow, cols_z), f32)

        def line(ref, first):
            return ref[:, first:first + cols_z].astype(f32)

        for x in range(depth_x):
            for y in range(rows_y):
                at = (x * rows_y + y) * cols_z
                centre = line(k_mine, at)
                beside = (
                    line(k_mine, at - plane) if x > 0 else line(halo_lo, y * cols_z),
                    line(k_mine, at + plane) if x < depth_x - 1 else line(halo_hi, y * cols_z),
                    line(k_mine, at - cols_z) if y > 0 else nothing,
                    line(k_mine, at + cols_z) if y < rows_y - 1 else nothing,
                    jnp.where(lane == 0, 0.0, pltpu.roll(centre, 1, 1)),
                    jnp.where(lane == cols_z - 1, 0.0, pltpu.roll(centre, cols_z - 1, 1)),
                )
                summed = nothing
                for face in range(6):
                    summed = summed + weight_ref[face:face + 1, at:at + cols_z] * (beside[face] - centre)
                lap[:, at:at + cols_z] = summed
        m_parts[me] = dot(lap[...].astype(bf16), joined(u_all[...]), ((1,), (1,)))
        for k in range(1, n_space):
            m_copy(k, me).start()

    def moment_sum():
        for k in range(1, n_space):
            m_copy(k, lax.rem(me - k + n_space, n_space)).wait_recv()
        total = m_parts[0]
        for k in range(1, n_space):
            total = total + m_parts[k]
        m_all[col] = total
        for k in range(1, n_samp):
            m_share(k, col).start()

    def moment_rows():
        for k in range(1, n_samp):
            m_share(k, lax.rem(col - k + n_samp, n_samp)).wait_recv()
        moment = m_all[...].reshape(rank, rank).T
        m_full[...] = core_ref[...].astype(bf16).astype(f32) + cell_scale * moment

    def finish_with(c, terms):
        spot = at_chunk(c)
        total = l_sum[chip, :, spot].astype(f32)
        for term in terms:
            total = total + term[:, spot].astype(f32)
        mine = m_full[pl.ds(pl.multiple_of(me * lane_width, lane_width), lane_width), :]
        high = mine.astype(bf16)
        low = (mine - high.astype(f32)).astype(bf16)
        v = joined(v_all[:, :, spot])
        l_out[:, spot] = dot(high, v, ((1,), (0,))) + dot(low, v, ((1,), (0,))) + cell_scale * total

    def finish_direct(c):
        for k in range(1, n_chip):
            l_copy(k, c).wait_recv()
        finish_with(c, [l_recv.at[k - 1] for k in range(1, n_chip)])

    def finish_line(c):
        for side in range(2):
            @pl.when(chip > 0 if side == 0 else chip < n_chip - 1)
            def _():
                l_line(side, chip, c).wait_recv()
        finish_with(c, [l_in_line.at[side, chip] for side in range(2)])

    for w in range(3, n_chip):
        wave(w)
    await_sibling(0)
    parts = chunk // tile

    def step(c, carry):
        compute(c, 0)
        wave(c + n_chip)

        @pl.when(c > 0)
        def _():
            chip_sum(c - 1)

        line_sums(c)
        for part in range(1, parts):
            compute(c, part)
        l_swap(c).start()

        for place, task in enumerate((stencil, moment_sum, moment_rows)):
            pl.when(c == min(place, n_chunks - 1))(task)

        @pl.when((c >= n_chip) & (c - n_chip < n_line))
        def _():
            finish_line(c - n_chip)

        @pl.when(c + 1 < n_chunks)
        def _():
            await_sibling(c + 1)

        return carry

    lax.fori_loop(0, n_chunks, step, 0)

    for first in range(0, cells, cell_tile):
        spot = slice(first, first + cell_tile)
        turned = (k_acc[spot, :].T * samp_scale).astype(bf16)
        for place in range(n_samp):
            k_part[place, :, spot] = turned[place * narrow:(place + 1) * narrow, :]
    for k in range(1, n_samp):
        k_copy(k).start()
    chip_sum(n_chunks - 1)
    for t in range(n_chunks, n_line + n_chip):
        line_sums(t)
    for c in range(max(0, n_chunks - n_chip), n_line):
        finish_line(c)
    for c in range(n_line, n_chunks - 1):
        finish_direct(c)
    for k in range(1, n_samp):
        k_copy(k).wait_recv()
    total = k_part[col].astype(f32)
    for k in range(1, n_samp):
        total = total + k_recv[k - 1].astype(f32)
    k_out[...] = k_mine[...].astype(f32) + step_size * (lap[...] + total)
    finish_direct(n_chunks - 1)

    for k in range(1, n_samp):
        u_copy(k, col).wait_send()
        m_share(k, col).wait_send()
        k_copy(k).wait_send()
    for k in range(1, n_space):
        m_copy(k, me).wait_send()

    @pl.when(me < n_space - 1)
    def _():
        halo_up().wait_send()

    @pl.when(me > 0)
    def _():
        halo_down().wait_send()

    def sent(c, carry):
        for side in range(2):
            for k in range(n_chip):
                @pl.when(held(side, k) & goes_on(side))
                def _():
                    v_line(side, k, c).wait_send()

                if k > 0:
                    @pl.when(held(side, k))
                    def _():
                        v_forward(side, k, c, core).wait_send()
        v_own(c, me).wait_send()
        l_swap(c).wait_send()

        @pl.when(c < n_line)
        def _():
            for side in range(2):
                for target in range(n_chip):
                    @pl.when(chip < target if side == 0 else chip > target)
                    def _():
                        l_line(side, target, c).wait_send()

        @pl.when(c >= n_line)
        def _():
            for k in range(1, n_chip):
                l_copy(k, c).wait_send()

        return carry

    lax.fori_loop(0, n_chunks, sent, 0)


def per_device(basis_u, basis_v, core_s, face_class, sample_class):
    n_space = lax.axis_size("space")
    n_samp = lax.axis_size("samp")
    narrow, depth_x, rows_y, cols_z = basis_u.shape
    rank = core_s.shape[0]
    lane_width, samples = basis_v.shape
    cells = depth_x * rows_y * cols_z
    plane = rows_y * cols_z
    n_chip = n_space // 2
    chunk = min(1024, samples)
    tile = min(512, chunk)
    cell_tile = min(512, cells)
    n_chunks = samples // chunk
    core_cols = lax.dynamic_slice_in_dim(
        core_s.astype(bf16).T, lax.axis_index("samp") * narrow, narrow, 0
    )
    weight = 0.25 * jnp.exp2(face_class.astype(f32)).reshape(face_class.shape[0], cells)
    dims = (n_space, n_samp, n_chunks, chunk, tile, cell_tile, depth_x, rows_y, cols_z)
    dma = pltpu.SemaphoreType.DMA
    vmem = pl.BlockSpec(memory_space=pltpu.VMEM)
    k_new, l_new = pl.pallas_call(
        functools.partial(kernel, dims),
        out_shape=(
            jax.ShapeDtypeStruct((narrow, cells), f32),
            jax.ShapeDtypeStruct((lane_width, samples), f32),
        ),
        in_specs=[vmem] * 6,
        out_specs=(vmem, vmem),
        scratch_shapes=[
            pltpu.VMEM((n_samp, narrow, cells), bf16),
            pltpu.VMEM((n_space, lane_width, samples), bf16),
            pltpu.VMEM((cells, rank), bf16),
            pltpu.VMEM((narrow, cells), bf16),
            pltpu.VMEM((narrow, plane), bf16),
            pltpu.VMEM((narrow, plane), bf16),
            pltpu.VMEM((narrow, cells), f32),
            pltpu.VMEM((cells, rank), f32),
            pltpu.VMEM((cells, tile), bf16),
            pltpu.VMEM((n_space, narrow, rank), f32),
            pltpu.VMEM((n_samp, narrow, rank), f32),
            pltpu.VMEM((rank, rank), f32),
            pltpu.VMEM((2, n_chip, lane_width, samples), bf16),
            pltpu.VMEM((n_chip, lane_width, samples), bf16),
            pltpu.VMEM((n_chip, lane_width, samples), bf16),
            pltpu.VMEM((n_chip - 1, lane_width, samples), bf16),
            pltpu.VMEM((2, n_chip, lane_width, samples), bf16),
            pltpu.VMEM((2, n_chip, lane_width, samples), bf16),
            pltpu.VMEM((n_samp, narrow, cells), bf16),
            pltpu.VMEM((n_samp - 1, narrow, cells), bf16),
            dma((n_samp,)), dma((n_samp,)),
            dma((2, n_chip, n_chunks)), dma((2, n_chip + 1, n_chunks)),
            dma((2, n_chip, n_chunks)), dma((2, n_chip, n_chunks)),
            dma((2,)), dma((2,)),
            dma((n_space,)), dma((n_space,)),
            dma((n_samp,)), dma((n_samp,)),
            dma((n_chunks,)), dma((n_chunks,)),
            dma((n_chip, n_chunks)), dma((n_chip, n_chunks)),
            dma((n_samp,)), dma((n_samp,)),
            dma((2, n_chip, n_chunks)), dma((2, n_chip, n_chunks)),
        ],
        compiler_params=pltpu.CompilerParams(
            collective_id=0, has_side_effects=True, vmem_limit_bytes=48 * 1024 * 1024
        ),
        cost_estimate=pl.CostEstimate(
            flops=6 * cells * samples * rank, bytes_accessed=2 * rank * samples, transcendentals=0
        ),
    )(
        basis_u.reshape(narrow, cells), basis_v, core_s, core_cols, weight,
        sample_class.reshape(1, samples),
    )
    return (k_new.reshape(narrow, depth_x, rows_y, cols_z), l_new)


def solution(mesh):
    placed = (
        P("samp", "space", None, None),
        P("space", "samp"),
        P(),
        P(None, "space", None, None),
        P("samp"),
    )
    return jax.shard_map(
        per_device,
        mesh=mesh,
        in_specs=placed,
        out_specs=(P("samp", "space", None, None), P("space", "samp")),
        check_vma=False,
    )
```

```python
import functools

import jax
import jax.numpy as jnp
from jax import lax
from jax.experimental import pallas as pl
from jax.experimental.pallas import tpu as pltpu
from jax.sharding import PartitionSpec as P

step_size = 0.1
f32 = jnp.float32
bf16 = jnp.bfloat16


def dot(a, b, dims):
    return lax.dot_general(a, b, (dims, ((), ())), preferred_element_type=f32)


def joined(blocks):
    n, rows, columns = blocks.shape
    if rows % 16 == 0:
        return blocks.reshape(n * rows, columns)
    return blocks.astype(f32).reshape(n * rows, columns).astype(blocks.dtype)


def kernel(
    dims, u_ref, v_ref, core_ref, core_cols_ref, weight_ref, class_ref,
    k_out, l_out,
    u_all, v_all, k_rows, k_mine, halo_lo, halo_hi, lap, k_acc, react,
    m_parts, m_all, m_full, l_part, l_sib, l_sum, l_recv, l_out_line, l_in_line, k_part, k_recv,
    u_s, u_r, v_s, v_r, w_s, w_r, h_s, h_r, m_s, m_r, n_s, n_r,
    a_s, a_r, b_s, b_r, c_s, c_r, d_s, d_r,
):
    n_space, n_samp, n_chunks, chunk, tile, cell_tile, depth_x, rows_y, cols_z = dims
    n_chip = n_space // 2
    n_line = max(0, n_chunks - 2)
    narrow, cells = u_ref.shape
    lane_width, samples = v_ref.shape
    rank = n_samp * narrow
    plane = rows_y * cols_z
    cell_scale = step_size * rank / (cells * n_space)
    samp_scale = rank / (samples * n_samp)

    me = lax.axis_index("space")
    col = lax.axis_index("samp")
    chip, core = me // 2, me % 2
    other = 1 - core

    def space_peer(k):
        return lax.rem(me + k, n_space)

    def samp_peer(k):
        return lax.rem(col + k, n_samp)

    def chip_peer(k):
        return lax.rem(chip + k, n_chip)

    def chip_before(k):
        return lax.rem(chip - k + n_chip, n_chip)

    def remote(src, dst, send, recv, where):
        return pltpu.make_async_remote_copy(
            src_ref=src, dst_ref=dst, send_sem=send, recv_sem=recv,
            device_id=where, device_id_type=pl.DeviceIdType.MESH,
        )

    def at_chunk(c):
        return pl.ds(pl.multiple_of(c * chunk, chunk), chunk)

    def to_sibling():
        return {"space": chip * 2 + other}

    def u_copy(k, slot):
        return remote(u_ref, u_all.at[slot], u_s.at[k], u_r.at[k], {"samp": samp_peer(k)})

    def toward(side):
        return lax.rem(chip + (1 if side == 0 else n_chip - 1), n_chip)

    def held(side, k):
        return chip >= k if side == 0 else chip + k < n_chip

    def goes_on(side):
        return chip < n_chip - 1 if side == 0 else chip > 0

    def origin(side, k):
        return lax.rem(chip + (n_chip - k if side == 0 else k), n_chip)

    def v_line(side, k, c):
        slot = origin(side, k) * 2 + core
        block = v_all.at[slot, :, at_chunk(c)]
        return remote(
            v_ref.at[:, at_chunk(c)] if k == 0 else block, block,
            v_s.at[side, k, c], v_r.at[side, k + 1, c], {"space": toward(side) * 2 + core},
        )

    def v_arrival(side, k, c):
        block = v_all.at[origin(side, k) * 2 + core, :, at_chunk(c)]
        return remote(
            block, block, v_s.at[side, k - 1, c], v_r.at[side, k, c],
            {"space": toward(side) * 2 + core},
        )

    def v_own(c, slot):
        return remote(
            v_ref.at[:, at_chunk(c)], v_all.at[slot, :, at_chunk(c)],
            w_s.at[0, 0, c], w_r.at[0, 0, c], to_sibling(),
        )

    def v_forward(side, k, c, which):
        block = v_all.at[origin(side, k) * 2 + which, :, at_chunk(c)]
        return remote(block, block, w_s.at[side, k, c], w_r.at[side, k, c], to_sibling())

    def l_line(side, target, c):
        return remote(
            l_out_line.at[side, target, :, at_chunk(c)], l_in_line.at[side, target, :, at_chunk(c)],
            d_s.at[side, target, c], d_r.at[side, target, c], {"space": toward(side) * 2 + core},
        )

    def l_swap(c):
        return remote(
            l_part.at[other, :, :, at_chunk(c)], l_sib.at[:, :, at_chunk(c)],
            a_s.at[c], a_r.at[c], to_sibling(),
        )

    def l_copy(k, c):
        return remote(
            l_sum.at[chip_peer(k), :, at_chunk(c)], l_recv.at[k - 1, :, at_chunk(c)],
            b_s.at[k, c], b_r.at[k, c], {"space": chip_peer(k) * 2 + core},
        )

    def m_copy(k, slot):
        return remote(m_parts.at[me], m_parts.at[slot], m_s.at[k], m_r.at[k], {"space": space_peer(k)})

    def m_share(k, slot):
        return remote(m_all.at[col], m_all.at[slot], n_s.at[k], n_r.at[k], {"samp": samp_peer(k)})

    def k_copy(k):
        return remote(k_part.at[samp_peer(k)], k_recv.at[k - 1], c_s.at[k], c_r.at[k], {"samp": samp_peer(k)})

    def halo_up():
        return remote(k_mine.at[:, pl.ds(cells - plane, plane)], halo_lo, h_s.at[0], h_r.at[0], {"space": space_peer(1)})

    def halo_down():
        return remote(k_mine.at[:, pl.ds(0, plane)], halo_hi, h_s.at[1], h_r.at[1], {"space": space_peer(n_space - 1)})

    barrier = pltpu.get_barrier_semaphore()
    for k in range(1, n_space):
        pl.semaphore_signal(barrier, inc=1, device_id={"space": space_peer(k)}, device_id_type=pl.DeviceIdType.MESH)
    for k in range(1, n_samp):
        pl.semaphore_signal(barrier, inc=1, device_id={"samp": samp_peer(k)}, device_id_type=pl.DeviceIdType.MESH)
    pl.semaphore_wait(barrier, n_space + n_samp - 2)

    for k in range(1, n_samp):
        u_copy(k, col).start()

    def wave(w):
        for k in range(n_chip):
            c = w - k

            @pl.when((c >= 0) & (c < n_chunks))
            def _():
                for side in range(2):
                    if k > 0:
                        @pl.when(held(side, k))
                        def _():
                            v_arrival(side, k, c).wait_recv()

                            @pl.when(goes_on(side))
                            def _():
                                v_line(side, k, c).start()

                            v_forward(side, k, c, core).start()
                    else:
                        @pl.when(goes_on(side))
                        def _():
                            v_line(side, k, c).start()
                if k == 0:
                    v_own(c, me).start()

    wave(0)
    u_all[col] = u_ref[...]
    v_all[me] = v_ref[...]
    k_acc[...] = jnp.zeros_like(k_acc)
    for side in range(2):
        @pl.when(chip == (0 if side == 0 else n_chip - 1))
        def _():
            l_in_line[side] = jnp.zeros_like(l_in_line[side])
    wave(1)
    wave(2)

    for k in range(1, n_samp):
        u_copy(k, lax.rem(col - k + n_samp, n_samp)).wait_recv()

    core_b = core_ref[...].astype(bf16)
    for first in range(0, cells, cell_tile):
        spot = slice(first, first + cell_tile)
        u_tile = joined(u_all[:, :, spot])
        k_rows[spot, :] = dot(u_tile, core_b, ((0,), (0,))).astype(bf16)
        k_mine[:, spot] = dot(core_cols_ref[...], u_tile, ((1,), (0,))).astype(bf16)

    @pl.when(me < n_space - 1)
    def _():
        halo_up().start()

    @pl.when(me > 0)
    def _():
        halo_down().start()

    def await_sibling(c):
        v_own(c, chip * 2 + other).wait_recv()
        for side in range(2):
            for k in range(1, n_chip):
                @pl.when(held(side, k))
                def _():
                    v_forward(side, k, c, other).wait_recv()

    def compute(c, part):
        spot = pl.ds(pl.multiple_of(c * chunk + part * tile, tile), tile)
        v = joined(v_all[:, :, spot])
        growth = 0.5 + 0.5 * class_ref[:, spot].astype(f32)
        for first in range(0, cells, cell_tile):
            rows = slice(first, first + cell_tile)
            field = dot(k_rows[rows, :], v, ((1,), (0,)))
            reaction = (field * (growth - field * field)).astype(bf16)
            react[rows, :] = reaction
            k_acc[rows, :] += dot(reaction, v, ((1,), (1,)))
        u_full = joined(u_all[...])
        onto_u = dot(u_full, react[...], ((1,), (0,))).astype(bf16)
        for place in range(n_chip):
            for side in range(2):
                row = (2 * place + side) * lane_width
                l_part[side, place, :, spot] = onto_u[row:row + lane_width, :]

    def chip_sum(c):
        l_swap(c).wait_recv()
        spot = at_chunk(c)
        l_sum[:, :, spot] = (l_part[core, :, :, spot].astype(f32) + l_sib[:, :, spot].astype(f32)).astype(bf16)

        @pl.when(c >= n_line)
        def _():
            for k in range(1, n_chip):
                l_copy(k, c).start()

    def line_sums(t):
        for side in range(2):
            c = t - 1 - (chip if side == 0 else n_chip - 1 - chip)

            @pl.when((c >= 0) & (c < n_line))
            def _():
                spot = at_chunk(c)
                for target in range(n_chip):
                    @pl.when(chip < target if side == 0 else chip > target)
                    def _():
                        @pl.when(chip > 0 if side == 0 else chip < n_chip - 1)
                        def _():
                            l_line(side, target, c).wait_recv()

                        l_out_line[side, target, :, spot] = (
                            l_sum[target, :, spot].astype(f32) + l_in_line[side, target, :, spot].astype(f32)
                        ).astype(bf16)
                        l_line(side, target, c).start()

    def stencil():
        @pl.when(me > 0)
        def _():
            halo_up().wait_recv()

        @pl.when(me == 0)
        def _():
            halo_lo[...] = jnp.zeros_like(halo_lo)

        @pl.when(me < n_space - 1)
        def _():
            halo_down().wait_recv()

        @pl.when(me == n_space - 1)
        def _():
            halo_hi[...] = jnp.zeros_like(halo_hi)

        lane = lax.broadcasted_iota(jnp.int32, (narrow, cols_z), 1)
        nothing = jnp.zeros((narrow, cols_z), f32)

        def line(ref, first):
            return ref[:, first:first + cols_z].astype(f32)

        for x in range(depth_x):
            for y in range(rows_y):
                at = (x * rows_y + y) * cols_z
                centre = line(k_mine, at)
                beside = (
                    line(k_mine, at - plane) if x > 0 else line(halo_lo, y * cols_z),
                    line(k_mine, at + plane) if x < depth_x - 1 else line(halo_hi, y * cols_z),
                    line(k_mine, at - cols_z) if y > 0 else nothing,
                    line(k_mine, at + cols_z) if y < rows_y - 1 else nothing,
                    jnp.where(lane == 0, 0.0, pltpu.roll(centre, 1, 1)),
                    jnp.where(lane == cols_z - 1, 0.0, pltpu.roll(centre, cols_z - 1, 1)),
                )
                summed = nothing
                for face in range(6):
                    summed = summed + weight_ref[face:face + 1, at:at + cols_z] * (beside[face] - centre)
                lap[:, at:at + cols_z] = summed
        m_parts[me] = dot(lap[...].astype(bf16), joined(u_all[...]), ((1,), (1,)))
        for k in range(1, n_space):
            m_copy(k, me).start()

    def moment_sum():
        for k in range(1, n_space):
            m_copy(k, lax.rem(me - k + n_space, n_space)).wait_recv()
        total = m_parts[0]
        for k in range(1, n_space):
            total = total + m_parts[k]
        m_all[col] = total
        for k in range(1, n_samp):
            m_share(k, col).start()

    def moment_rows():
        for k in range(1, n_samp):
            m_share(k, lax.rem(col - k + n_samp, n_samp)).wait_recv()
        moment = m_all[...].reshape(rank, rank).T
        m_full[...] = core_ref[...].astype(bf16).astype(f32) + cell_scale * moment

    def finish_with(c, terms):
        spot = at_chunk(c)
        total = l_sum[chip, :, spot].astype(f32)
        for term in terms:
            total = total + term[:, spot].astype(f32)
        mine = m_full[pl.ds(pl.multiple_of(me * lane_width, lane_width), lane_width), :]
        high = mine.astype(bf16)
        low = (mine - high.astype(f32)).astype(bf16)
        v = joined(v_all[:, :, spot])
        l_out[:, spot] = dot(high, v, ((1,), (0,))) + dot(low, v, ((1,), (0,))) + cell_scale * total

    def finish_direct(c):
        for k in range(1, n_chip):
            l_copy(k, c).wait_recv()
        finish_with(c, [l_recv.at[k - 1] for k in range(1, n_chip)])

    def finish_line(c):
        for side in range(2):
            @pl.when(chip > 0 if side == 0 else chip < n_chip - 1)
            def _():
                l_line(side, chip, c).wait_recv()
        finish_with(c, [l_in_line.at[side, chip] for side in range(2)])

    for w in range(3, n_chip):
        wave(w)
    await_sibling(0)
    parts = chunk // tile

    def step(c, carry):
        compute(c, 0)
        wave(c + n_chip)

        @pl.when(c > 0)
        def _():
            chip_sum(c - 1)

        line_sums(c)
        for part in range(1, parts):
            compute(c, part)
        l_swap(c).start()

        for place, task in ((0, stencil), (2, moment_sum), (4, moment_rows)):
            pl.when(c == min(place, n_chunks - 1))(task)

        @pl.when((c >= n_chip) & (c - n_chip < n_line))
        def _():
            finish_line(c - n_chip)

        @pl.when(c + 1 < n_chunks)
        def _():
            await_sibling(c + 1)

        return carry

    lax.fori_loop(0, n_chunks, step, 0)

    for first in range(0, cells, cell_tile):
        spot = slice(first, first + cell_tile)
        turned = (k_acc[spot, :].T * samp_scale).astype(bf16)
        for place in range(n_samp):
            k_part[place, :, spot] = turned[place * narrow:(place + 1) * narrow, :]
    for k in range(1, n_samp):
        k_copy(k).start()
    chip_sum(n_chunks - 1)
    for t in range(n_chunks, n_line + n_chip):
        line_sums(t)
    for c in range(max(0, n_chunks - n_chip), n_line):
        finish_line(c)
    for c in range(n_line, n_chunks - 1):
        finish_direct(c)
    for k in range(1, n_samp):
        k_copy(k).wait_recv()
    total = k_part[col].astype(f32)
    for k in range(1, n_samp):
        total = total + k_recv[k - 1].astype(f32)
    k_out[...] = k_mine[...].astype(f32) + step_size * (lap[...] + total)
    finish_direct(n_chunks - 1)

    for k in range(1, n_samp):
        u_copy(k, col).wait_send()
        m_share(k, col).wait_send()
        k_copy(k).wait_send()
    for k in range(1, n_space):
        m_copy(k, me).wait_send()

    @pl.when(me < n_space - 1)
    def _():
        halo_up().wait_send()

    @pl.when(me > 0)
    def _():
        halo_down().wait_send()

    def sent(c, carry):
        for side in range(2):
            for k in range(n_chip):
                @pl.when(held(side, k) & goes_on(side))
                def _():
                    v_line(side, k, c).wait_send()

                if k > 0:
                    @pl.when(held(side, k))
                    def _():
                        v_forward(side, k, c, core).wait_send()
        v_own(c, me).wait_send()
        l_swap(c).wait_send()

        @pl.when(c < n_line)
        def _():
            for side in range(2):
                for target in range(n_chip):
                    @pl.when(chip < target if side == 0 else chip > target)
                    def _():
                        l_line(side, target, c).wait_send()

        @pl.when(c >= n_line)
        def _():
            for k in range(1, n_chip):
                l_copy(k, c).wait_send()

        return carry

    lax.fori_loop(0, n_chunks, sent, 0)


def per_device(basis_u, basis_v, core_s, face_class, sample_class):
    n_space = lax.axis_size("space")
    n_samp = lax.axis_size("samp")
    narrow, depth_x, rows_y, cols_z = basis_u.shape
    rank = core_s.shape[0]
    lane_width, samples = basis_v.shape
    cells = depth_x * rows_y * cols_z
    plane = rows_y * cols_z
    n_chip = n_space // 2
    chunk = min(1024, samples)
    tile = min(512, chunk)
    cell_tile = min(512, cells)
    n_chunks = samples // chunk
    core_cols = lax.dynamic_slice_in_dim(
        core_s.astype(bf16).T, lax.axis_index("samp") * narrow, narrow, 0
    )
    weight = 0.25 * jnp.exp2(face_class.astype(f32)).reshape(face_class.shape[0], cells)
    dims = (n_space, n_samp, n_chunks, chunk, tile, cell_tile, depth_x, rows_y, cols_z)
    dma = pltpu.SemaphoreType.DMA
    vmem = pl.BlockSpec(memory_space=pltpu.VMEM)
    k_new, l_new = pl.pallas_call(
        functools.partial(kernel, dims),
        out_shape=(
            jax.ShapeDtypeStruct((narrow, cells), f32),
            jax.ShapeDtypeStruct((lane_width, samples), f32),
        ),
        in_specs=[vmem] * 6,
        out_specs=(vmem, vmem),
        scratch_shapes=[
            pltpu.VMEM((n_samp, narrow, cells), bf16),
            pltpu.VMEM((n_space, lane_width, samples), bf16),
            pltpu.VMEM((cells, rank), bf16),
            pltpu.VMEM((narrow, cells), bf16),
            pltpu.VMEM((narrow, plane), bf16),
            pltpu.VMEM((narrow, plane), bf16),
            pltpu.VMEM((narrow, cells), f32),
            pltpu.VMEM((cells, rank), f32),
            pltpu.VMEM((cells, tile), bf16),
            pltpu.VMEM((n_space, narrow, rank), f32),
            pltpu.VMEM((n_samp, narrow, rank), f32),
            pltpu.VMEM((rank, rank), f32),
            pltpu.VMEM((2, n_chip, lane_width, samples), bf16),
            pltpu.VMEM((n_chip, lane_width, samples), bf16),
            pltpu.VMEM((n_chip, lane_width, samples), bf16),
            pltpu.VMEM((n_chip - 1, lane_width, samples), bf16),
            pltpu.VMEM((2, n_chip, lane_width, samples), bf16),
            pltpu.VMEM((2, n_chip, lane_width, samples), bf16),
            pltpu.VMEM((n_samp, narrow, cells), bf16),
            pltpu.VMEM((n_samp - 1, narrow, cells), bf16),
            dma((n_samp,)), dma((n_samp,)),
            dma((2, n_chip, n_chunks)), dma((2, n_chip + 1, n_chunks)),
            dma((2, n_chip, n_chunks)), dma((2, n_chip, n_chunks)),
            dma((2,)), dma((2,)),
            dma((n_space,)), dma((n_space,)),
            dma((n_samp,)), dma((n_samp,)),
            dma((n_chunks,)), dma((n_chunks,)),
            dma((n_chip, n_chunks)), dma((n_chip, n_chunks)),
            dma((n_samp,)), dma((n_samp,)),
            dma((2, n_chip, n_chunks)), dma((2, n_chip, n_chunks)),
        ],
        compiler_params=pltpu.CompilerParams(
            collective_id=0, has_side_effects=True, vmem_limit_bytes=48 * 1024 * 1024
        ),
        cost_estimate=pl.CostEstimate(
            flops=6 * cells * samples * rank, bytes_accessed=2 * rank * samples, transcendentals=0
        ),
    )(
        basis_u.reshape(narrow, cells), basis_v, core_s, core_cols, weight,
        sample_class.reshape(1, samples),
    )
    return (k_new.reshape(narrow, depth_x, rows_y, cols_z), l_new)


def solution(mesh):
    placed = (
        P("samp", "space", None, None),
        P("space", "samp"),
        P(),
        P(None, "space", None, None),
        P("samp"),
    )
    return jax.shard_map(
        per_device,
        mesh=mesh,
        in_specs=placed,
        out_specs=(P("samp", "space", None, None), P("space", "samp")),
        check_vma=False,
    )
```
